768 devices in a mesh: row: 192 (over y, x, z_lo), col: 4 (over z_hi, core).
Axes of the slice: x: 4, y: 8, z: 12 (z_hi: 2, z_lo: 6; z = z_hi * 6 + z_lo), core: 2. Of those that a mesh axis runs over, the one named last changes fastest.
Arguments:
- start_rows: bfloat16 [98304, 128], P('row'), may hold values from -3 to 3
- col_factors: bfloat16 [24576, 128], P(('row', 'col')), as said below
- block_rows: int32 [192, 4, 32], P('row', 'col'), may hold values from 0 to 3
- block_cols: int32 [192, 4, 32], P('row', 'col'), may hold values from 0 to 47
- block_masks: int32 [192, 4, 32, 128, 128], P('row', 'col'), may hold values 0 or 1
- block_counts: int32 [192, 4], P('row', 'col'), may hold values from 1 to 32, as said below
Outputs:
- solution: bfloat16 [98304, 128], P(('row', 'col'))
- residual: float32 [98304, 128], P(('row', 'col'))
The draws below stay inside these ranges and needn't reach their ends.
Inputs may be any that keep to these rules, and one draw needn't show every extreme that they name: `block_counts`: entries past a list's count are ignored; in every draw some list has exactly 32 live slots. `col_factors`: column factor rows have scales spread over a wide range.
All inputs are finite; a program needn't handle non-finite values. No bound on the sum of `block_masks` on one device may be relied on, other than what follows from the above.
Results may differ from the reference program's by a relative error of at most 0.04.
Values may be sent and summed in bfloat16 or wider, within the bound.
No kernel may reach another device: no remote copies, remote signals or barrier semaphores. Data moves between devices by JAX's collectives and lax.ppermute only.
A program may use at most 32 MiB of HBM per device.

```python
import math
import jax
import jax.numpy as jnp
from jax import lax

K = 128
BLK = 128
R_DEV = 512
VP = 32
NB = 32
ITERS = 3
NROWS = 98304
NCOL = 24576
RB = 4
CB = 48
N_ROW = 192
N_COL = 4


def draw_col_factors(key, part):
    key = jax.random.fold_in(key, 11)
    first, second, third = jax.random.split(key, 3)
    position = jnp.arange(NCOL, dtype=jnp.float32)[:, None] / NCOL
    base = jax.random.normal(first, (NCOL, K), jnp.float32)
    spread = jax.random.uniform(second, (NCOL, 1), jnp.float32, 0.0, 1.0)
    feature = jax.random.uniform(third, (1, K), jnp.float32, 0.0, 0.5)
    scale = 0.3 * jnp.power(10.0, spread) * jnp.power(3.0, position) * jnp.power(10.0, feature - 0.25)
    return (base * scale / math.sqrt(K)).astype(jnp.bfloat16)


def draw_block_counts(key, part):
    key = jax.random.fold_in(key, 23)
    first, second = jax.random.split(key, 2)
    counts = jax.random.randint(first, (N_ROW * N_COL,), 1, NB + 1)
    chosen = jax.random.randint(second, (), 0, N_ROW * N_COL)
    counts = counts.at[chosen].set(NB)
    return counts.reshape(N_ROW, N_COL).astype(jnp.int32)


def with_ends(array, own_key, smallest, largest):
    shape = array.shape
    spot = [jax.random.randint(jax.random.fold_in(own_key, axis), (), 0, shape[axis]) for axis in range(len(shape))]
    array = array.at[tuple(spot)].set(smallest)
    longest = shape.index(max(shape))
    spot[longest] = (spot[longest] + 1) % shape[longest]
    return array.at[tuple(spot)].set(largest)


def steps_of(own_key, extent, cuts, smallest, high):
    def one(dim, blocks):
        steps = jax.random.uniform(jax.random.fold_in(jax.random.fold_in(own_key, 6), dim), (blocks,), jnp.float32, smallest / len(cuts), high / len(cuts))
        return jnp.repeat(jnp.exp(steps), extent[dim] // blocks).reshape((-1,) + (1,) * (len(extent) - dim - 1))

    gain = one(*cuts[0])
    for cut in cuts[1:]:
        gain = gain * one(*cut)
    return gain


def centred(own_key, dims, scale, reach, pieces=(), held_as=jnp.bfloat16):
    level = steps_of(own_key, dims, pieces, -0.22, 0.18) if pieces else 1.0
    drawn = jax.random.normal(own_key, dims, jnp.float32) * scale * level
    return jnp.minimum(jnp.maximum(drawn, -reach), reach).astype(held_as)


def setup_inputs(seed: int = 0) -> dict:
    key_of = jax.random.split(jax.random.key(seed), 7)
    start_rows = centred(key_of[0], (NROWS, K), 0.5, 3.0, ((0, 192),))
    col_factors = draw_col_factors(jax.random.fold_in(key_of[6], 71), 0)
    block_rows = with_ends(jax.random.randint(key_of[2], (N_ROW, N_COL, NB), 0, RB), jax.random.fold_in(key_of[2], 1), 0, RB - 1).astype(jnp.int32)
    block_cols = with_ends(jax.random.randint(key_of[3], (N_ROW, N_COL, NB), 0, CB), jax.random.fold_in(key_of[3], 1), 0, CB - 1).astype(jnp.int32)
    block_masks = with_ends((jax.random.randint(key_of[4], (N_ROW, N_COL, NB, BLK, BLK), 0, 3) < 1).astype(jnp.int32), jax.random.fold_in(key_of[4], 1), 0, 1)
    block_counts = draw_block_counts(jax.random.fold_in(key_of[6], 71), 0)
    return {"start_rows": start_rows, "col_factors": col_factors, "block_rows": block_rows, "block_cols": block_cols, "block_masks": block_masks, "block_counts": block_counts}


CONFIDENCE = 2.0
REGULARIZE = 0.5
EPSILON = 1e-6


def block_sum(factor, col_shard, row_ids, col_ids, edge_masks, live_count, opening):
    slots = row_ids.shape[0]
    row_blocks = factor.reshape(-1, BLK, K)[row_ids].astype(jnp.float32)
    col_blocks = col_shard.reshape(-1, BLK, K)[col_ids].astype(jnp.float32)
    scores = jnp.einsum('nik,njk->nij', row_blocks, col_blocks)
    live = ((jnp.arange(slots) < live_count)[:, None, None] & (edge_masks > 0)).astype(jnp.float32)
    if opening:
        weights = ((1.0 + CONFIDENCE) - CONFIDENCE * scores) * live
    else:
        weights = CONFIDENCE * scores * live
    weights = lax.optimization_barrier(weights.astype(jnp.bfloat16)).astype(jnp.float32)
    terms = jnp.einsum('nij,njk->nik', weights, col_blocks)
    placer = (row_ids[None, :] == jnp.arange(factor.shape[0] // BLK)[:, None]).astype(jnp.float32)
    return jnp.einsum('rn,nik->rik', placer, terms).reshape(factor.shape[0], K)


def sparse_apply(factor, col_factors, block_rows, block_cols, block_masks, block_counts, opening):
    shards = col_factors.reshape(N_ROW, N_COL, VP, K).transpose(1, 0, 2, 3).reshape(N_COL, N_ROW * VP, K)
    slabs = factor.reshape(N_ROW, R_DEV, K)

    def per_slab(items):
        slab_rows, row_ids, col_ids, edge_masks, live_count = items
        summed = jnp.zeros((R_DEV, K), jnp.float32)
        for group in range(N_COL):
            summed = summed + block_sum(slab_rows, shards[group], row_ids[group], col_ids[group],
                                        edge_masks[group], live_count[group], opening)
        return summed

    result = lax.map(per_slab, (slabs, block_rows, block_cols, block_masks, block_counts))
    return result.reshape(NROWS, K)


def reference(start_rows, col_factors, block_rows, block_cols, block_masks, block_counts):
    gramian = jnp.dot(col_factors.T, col_factors, preferred_element_type=jnp.float32)
    gravity = K / NCOL

    def dense(matrix):
        return gravity * jnp.dot(matrix, gramian, precision=lax.Precision.HIGHEST) + REGULARIZE * matrix

    initial = sparse_apply(start_rows, col_factors, block_rows, block_cols, block_masks, block_counts, True)
    solution = start_rows.astype(jnp.float32)
    residual = initial - dense(solution)
    direction = residual
    norm_now = jnp.sum(residual * residual, axis=1, keepdims=True)
    for step in range(ITERS):
        image = dense(direction) + sparse_apply(direction.astype(jnp.bfloat16), col_factors, block_rows,
                                                block_cols, block_masks, block_counts, False)
        step_size = norm_now / (jnp.sum(direction * image, axis=1, keepdims=True) + EPSILON)
        solution = solution + step_size * direction
        residual = residual - step_size * image
        norm_next = jnp.sum(residual * residual, axis=1, keepdims=True)
        direction = residual + (norm_next / (norm_now + EPSILON)) * direction
        norm_now = norm_next
    return solution.astype(jnp.bfloat16), residual
```

```python
import jax
import jax.numpy as jnp
from jax import lax
from jax.experimental import pallas as pl
from jax.experimental.pallas import tpu as pltpu
from jax.sharding import Mesh, PartitionSpec as P

ITERS = 3
CONFIDENCE = 2.0
REGULARIZE = 0.5
EPSILON = 1e-06

ROW = ("y", "x", "zl")
COL = ("zh", "core")
SIZES = {"y": 8, "x": 4, "zl": 6, "zh": 2, "core": 2}

BLK = 128
K = 128
NB = 32
PIECE = 2 * BLK
STRIDE = NB
TRIPS = 4 * STRIDE
SHIFT = 64
VMEM_LIMIT = 40 * 1024 * 1024


def lists_kernel(ids_ref, out_ref):
    core = lax.axis_index("core")

    def clear(i, carry):
        out_ref[i] = NB * SHIFT
        return carry

    lax.fori_loop(0, 4 * STRIDE, clear, 0, unroll=8)
    longest = jnp.int32(0)
    for group in range(2):
        holder = core if group == 0 else 1 - core
        live = ids_ref[holder, 2 * NB]

        def place(slot, ends, holder=holder, group=group):
            low, high = ends
            row = ids_ref[holder, slot]
            entry = slot * SHIFT + ids_ref[holder, NB + slot]
            mine = lax.rem(row, 2) == core
            upper = row >= 2

            @pl.when(mine)
            def _():
                out_ref[jnp.where(upper, (2 * group + 1) * STRIDE + high, 2 * group * STRIDE + low)] = entry

            low = low + jnp.where(mine & jnp.logical_not(upper), 1, 0)
            high = high + jnp.where(mine & upper, 1, 0)
            return low, high

        low, high = lax.fori_loop(0, live, place, (jnp.int32(0), jnp.int32(0)))
        longest = jnp.maximum(longest, jnp.maximum(low, high))
    out_ref[TRIPS] = lax.div(longest + 1, 2)


def gram_of(v_ref):
    step = 512

    def body(i, total):
        block = v_ref[pl.ds(pl.multiple_of(i * step, step), step), :]
        return total + lax.dot_general(
            block, block, (((0,), (0,)), ((), ())), preferred_element_type=jnp.float32
        )

    return lax.fori_loop(0, v_ref.shape[0] // step, body, jnp.zeros((K, K), jnp.float32))


def gram_kernel(v_ref, out_ref):
    out_ref[...] = gram_of(v_ref)


def add_sparse(lists_ref, x_ref, v_refs, m_refs, out_ref, opening):
    def body(i, carry):
        for r in range(2):
            cols = []
            masks = []
            for g in range(2):
                for k in range(2):
                    entry = lists_ref[(2 * g + r) * STRIDE + 2 * i + k]
                    slot = lax.div(entry, SHIFT)
                    start = pl.multiple_of(lax.rem(entry, SHIFT) * BLK, BLK)
                    cols.append(v_refs[g][pl.ds(start, BLK), :])
                    masks.append(m_refs[g][slot])
            block = jnp.concatenate(cols, axis=0)
            mask = jnp.concatenate(masks, axis=1)
            rows = x_ref[pl.ds(r * BLK, BLK), :]
            scores = lax.dot_general(
                rows, block, (((1,), (1,)), ((), ())), preferred_element_type=jnp.float32
            )
            if opening:
                scores = (1.0 + CONFIDENCE) / CONFIDENCE - scores
            weights = scores.astype(jnp.bfloat16) * mask
            out_ref[pl.ds(r * BLK, BLK), :] += jnp.dot(
                weights, block, preferred_element_type=jnp.float32
            )
        return carry

    lax.fori_loop(0, lists_ref[TRIPS], body, 0)


def exact_dot(a, b):
    return jnp.dot(a, b, precision=lax.Precision.HIGHEST, preferred_element_type=jnp.float32)


def init_kernel(gravity, lists_ref, x_ref, v0, v1, m0, m1, own_gram, part_ref, gram_ref):
    gram = gravity * (own_gram[...] + gram_of(v1))
    gram_ref[...] = gram
    part_ref[...] = -exact_dot(x_ref[...].astype(jnp.float32), gram)
    add_sparse(lists_ref, x_ref, (v0, v1), (m0, m1), part_ref, True)


def row_sum(a):
    return jnp.sum(a, axis=1, keepdims=True)


def advance(both, direction, residual, sol):
    image = both + REGULARIZE * direction
    norm_now = row_sum(residual * residual)
    step = norm_now / (row_sum(direction * image) + EPSILON)
    sol = sol + step * direction
    residual = residual - step * image
    return sol, residual, norm_now


def image_part(lists_ref, d, low_ref, v0, v1, m0, m1, gram_ref, part_ref):
    low_ref[...] = d.astype(jnp.bfloat16)
    part_ref[...] = exact_dot(d, gram_ref[...])
    add_sparse(lists_ref, low_ref, (v0, v1), (m0, m1), part_ref, False)


def start_kernel(lists_ref, both_ref, x_ref, v0, v1, m0, m1, gram_ref, res_ref, part_ref, low_ref):
    residual = both_ref[:PIECE] + both_ref[PIECE:] - REGULARIZE * x_ref[...].astype(jnp.float32)
    res_ref[...] = residual
    image_part(lists_ref, residual, low_ref, v0, v1, m0, m1, gram_ref, part_ref)


def step_kernel(
    lists_ref, both_ref, sol_in, res_in, dir_in, v0, v1, m0, m1, gram_ref,
    sol_ref, res_ref, dir_ref, part_ref, low_ref,
):
    direction = dir_in[...]
    sol, residual, norm_now = advance(
        both_ref[:PIECE] + both_ref[PIECE:], direction, res_in[...], sol_in[...].astype(jnp.float32)
    )
    sol_ref[...] = sol
    res_ref[...] = residual
    direction = residual + row_sum(residual * residual) / (norm_now + EPSILON) * direction
    dir_ref[...] = direction
    image_part(lists_ref, direction, low_ref, v0, v1, m0, m1, gram_ref, part_ref)


def last_kernel(both_ref, sol_in, res_in, dir_in, sol_ref, res_ref):
    start = pl.multiple_of(lax.axis_index("zh") * BLK, BLK)
    mine = pl.ds(start, BLK)
    both = both_ref[mine, :] + both_ref[pl.ds(start + PIECE, BLK), :]
    sol, residual, _ = advance(both, dir_in[mine, :], res_in[mine, :], sol_in[mine, :])
    sol_ref[...] = sol.astype(jnp.bfloat16)
    res_ref[...] = residual


def on_chip(kernel, args, outs, scratch=(), smem=1):
    vmem = pl.BlockSpec(memory_space=pltpu.VMEM)
    scalar = pl.BlockSpec(memory_space=pltpu.SMEM)
    return pl.pallas_call(
        kernel,
        out_shape=[jax.ShapeDtypeStruct(shape, dtype) for shape, dtype in outs],
        in_specs=[scalar] * smem + [vmem] * (len(args) - smem),
        out_specs=[vmem] * len(outs),
        scratch_shapes=list(scratch),
        compiler_params=pltpu.CompilerParams(vmem_limit_bytes=VMEM_LIMIT),
    )(*args)


def gather_by_exchange(block, axes):
    count = 1
    for axis in axes:
        count *= SIZES[axis]
    sent = jnp.broadcast_to(block[None], (count,) + block.shape)
    got = lax.all_to_all(sent, axes, 0, 0, tiled=True)
    return got.reshape(count * block.shape[0], block.shape[1])


def swap(value):
    return lax.ppermute(value, "core", [(0, 1), (1, 0)])


def per_device(start_rows, col_factors, block_rows, block_cols, block_masks, block_counts):
    f32, bf16 = jnp.float32, jnp.bfloat16
    core = lax.axis_index("core")
    gravity = K / (col_factors.shape[0] * 768)

    live = (jnp.arange(NB + 1) < block_counts[0, 0])[:, None, None]
    padded = jnp.pad(block_masks[0, 0], ((0, 1), (0, 0), (0, 0)))
    own_masks = jnp.where(live & (padded > 0), CONFIDENCE, 0.0).astype(bf16)
    other_masks = swap(own_masks)

    ids = jnp.concatenate(
        [block_rows[0, 0], block_cols[0, 0], jnp.broadcast_to(block_counts[0, 0], (2 * NB,))]
    )[None]
    ids = lax.all_gather(ids, "core", axis=0, tiled=True)
    lists = pl.pallas_call(
        lists_kernel,
        out_shape=jax.ShapeDtypeStruct((2 * TRIPS,), jnp.int32),
        in_specs=[pl.BlockSpec(memory_space=pltpu.SMEM)],
        out_specs=pl.BlockSpec(memory_space=pltpu.SMEM),
    )(ids)

    own = gather_by_exchange(gather_by_exchange(col_factors, ("zl",)), ("y", "x"))
    other = swap(own)
    (own_gram,) = on_chip(gram_kernel, (own,), [((K, K), f32)], smem=0)

    rows = lax.dynamic_slice_in_dim(start_rows.reshape(2, 2, BLK, K), core, 1, 1).reshape(PIECE, K)
    big = (own, other, own_masks, other_masks)
    whole = ((PIECE, K), f32)
    low = (pltpu.VMEM((PIECE, K), bf16),)

    def both(part):
        return lax.all_gather(part, "zh", axis=0, tiled=True)

    part, gram = on_chip(
        lambda *refs: init_kernel(gravity, *refs), (lists, rows) + big + (own_gram,), [whole, ((K, K), f32)]
    )
    residual, part = on_chip(
        start_kernel, (lists, both(part), rows) + big + (gram,), [whole] * 2, low
    )
    sol, direction = rows, residual
    for _ in range(ITERS - 1):
        sol, residual, direction, part = on_chip(
            step_kernel, (lists, both(part), sol, residual, direction) + big + (gram,), [whole] * 4, low
        )
    return tuple(
        on_chip(
            last_kernel, (both(part), sol, residual, direction), [((BLK, K), bf16), ((BLK, K), f32)], smem=0
        )
    )


def solution(mesh):
    fine = Mesh(mesh.devices.reshape(tuple(SIZES.values())), tuple(SIZES))
    placed = (
        P(ROW, None),
        P(ROW + COL, None),
        P(ROW, COL, None),
        P(ROW, COL, None),
        P(ROW, COL, None, None, None),
        P(ROW, COL),
    )
    return jax.shard_map(
        per_device,
        mesh=fine,
        in_specs=placed,
        out_specs=(P(ROW + COL, None), P(ROW + COL, None)),
        check_vma=False,
    )
```

```python
import jax
import jax.numpy as jnp
from jax import lax
from jax.experimental import pallas as pl
from jax.experimental.pallas import tpu as pltpu
from jax.sharding import Mesh, PartitionSpec as P

ITERS = 3
CONFIDENCE = 2.0
REGULARIZE = 0.5
EPSILON = 1e-06

ROW = ("y4", "y2", "y1", "x2", "x1", "z3", "z1")
COL = ("zh", "core")
SIZES = {"y4": 2, "y2": 2, "y1": 2, "x2": 2, "x1": 2, "z3": 3, "z1": 2, "zh": 2, "core": 2}
STAGES = (("y4", "y2", "z3"), ("y1", "x2", "x1", "z1"))

BLK = 128
K = 128
NB = 32
PIECE = 2 * BLK
STRIDE = NB
TRIPS = 4 * STRIDE
SHIFT = 64
VMEM_LIMIT = 40 * 1024 * 1024


def lists_kernel(ids_ref, out_ref):
    core = lax.axis_index("core")

    def clear(i, carry):
        out_ref[i] = NB * SHIFT
        return carry

    lax.fori_loop(0, 4 * STRIDE, clear, 0, unroll=8)
    longest = jnp.int32(0)
    for group in range(2):
        holder = core if group == 0 else 1 - core
        live = ids_ref[holder, 2 * NB]

        def place(slot, ends, holder=holder, group=group):
            low, high = ends
            row = ids_ref[holder, slot]
            entry = slot * SHIFT + ids_ref[holder, NB + slot]
            mine = lax.rem(row, 2) == core
            upper = row >= 2

            @pl.when(mine)
            def _():
                out_ref[jnp.where(upper, (2 * group + 1) * STRIDE + high, 2 * group * STRIDE + low)] = entry

            low = low + jnp.where(mine & jnp.logical_not(upper), 1, 0)
            high = high + jnp.where(mine & upper, 1, 0)
            return low, high

        low, high = lax.fori_loop(0, live, place, (jnp.int32(0), jnp.int32(0)))
        longest = jnp.maximum(longest, jnp.maximum(low, high))
    out_ref[TRIPS] = lax.div(longest + 1, 2)


def gram_of(v_ref):
    step = 2048

    def body(i, total):
        block = v_ref[pl.ds(pl.multiple_of(i * step, step), step), :]
        return total + lax.dot_general(
            block, block, (((0,), (0,)), ((), ())), preferred_element_type=jnp.float32
        )

    return lax.fori_loop(0, v_ref.shape[0] // step, body, jnp.zeros((K, K), jnp.float32))


def gram_kernel(v_ref, out_ref):
    out_ref[...] = gram_of(v_ref)


def picked(lists_ref, v_refs, m_refs, i, r, take):
    cols, masks = [], []
    for g in range(2):
        for k in range(take):
            entry = lists_ref[(2 * g + r) * STRIDE + take * i + k]
            start = pl.multiple_of((entry & (SHIFT - 1)) * BLK, BLK)
            cols.append(v_refs[g][pl.ds(start, BLK), :])
            masks.append(m_refs[g][entry >> 6])
    return jnp.concatenate(cols, axis=0), jnp.concatenate(masks, axis=1)


def weigh(rows, block, mask, opening):
    scores = lax.dot_general(
        rows, block, (((1,), (1,)), ((), ())), preferred_element_type=jnp.float32
    )
    if opening:
        scores = (1.0 + CONFIDENCE) / CONFIDENCE - scores
    return scores.astype(jnp.bfloat16) * mask


def add_sparse(lists_ref, x_ref, v_refs, m_refs, out_ref, opening):
    def body(i, carry):
        parts = []
        for r in range(2):
            for h in range(2):
                block, mask = picked(lists_ref, v_refs, m_refs, 2 * i + h, r, 2)
                parts.append((r, block, weigh(x_ref[pl.ds(r * BLK, BLK), :], block, mask, opening)))
        for r, block, weights in parts:
            out_ref[pl.ds(r * BLK, BLK), :] += jnp.dot(
                weights, block, preferred_element_type=jnp.float32
            )
        return carry

    lax.fori_loop(0, lax.div(lists_ref[TRIPS] + 1, 2), body, 0)


def halves(a):
    high = a.astype(jnp.bfloat16)
    return high, (a - high.astype(jnp.float32)).astype(jnp.bfloat16)


def exact_dot(a, b):
    a_high, a_low = halves(a)
    b_high, b_low = halves(b)
    left = jnp.concatenate([a_high, a_high, a_low], axis=1)
    right = jnp.concatenate([b_high, b_low, b_high], axis=0)
    return jnp.dot(left, right, preferred_element_type=jnp.float32)


def init_kernel(gravity, lists_ref, x_ref, v0, v1, m0, m1, own_gram, part_ref, gram_ref):
    gram = gravity * (own_gram[...] + gram_of(v1))
    gram_ref[...] = gram
    part_ref[...] = -exact_dot(x_ref[...].astype(jnp.float32), gram)
    add_sparse(lists_ref, x_ref, (v0, v1), (m0, m1), part_ref, True)


def row_sum(a):
    return jnp.sum(a, axis=1, keepdims=True)


def advance(both, direction, residual, sol):
    image = both + REGULARIZE * direction
    norm_now = row_sum(residual * residual)
    step = norm_now / (row_sum(direction * image) + EPSILON)
    sol = sol + step * direction
    residual = residual - step * image
    return sol, residual, norm_now


def image_part(lists_ref, d, low_ref, v0, v1, m0, m1, gram_ref, part_ref):
    low_ref[...] = d.astype(jnp.bfloat16)
    part_ref[...] = exact_dot(d, gram_ref[...])
    add_sparse(lists_ref, low_ref, (v0, v1), (m0, m1), part_ref, False)


def start_kernel(lists_ref, both_ref, x_ref, v0, v1, m0, m1, gram_ref, res_ref, part_ref, low_ref):
    residual = both_ref[:PIECE] + both_ref[PIECE:] - REGULARIZE * x_ref[...].astype(jnp.float32)
    res_ref[...] = residual
    image_part(lists_ref, residual, low_ref, v0, v1, m0, m1, gram_ref, part_ref)


def step_kernel(
    lists_ref, both_ref, sol_in, res_in, dir_in, v0, v1, m0, m1, gram_ref,
    sol_ref, res_ref, dir_ref, part_ref, low_ref,
):
    direction = dir_in[...]
    sol, residual, norm_now = advance(
        both_ref[:PIECE] + both_ref[PIECE:], direction, res_in[...], sol_in[...].astype(jnp.float32)
    )
    sol_ref[...] = sol
    res_ref[...] = residual
    direction = residual + row_sum(residual * residual) / (norm_now + EPSILON) * direction
    dir_ref[...] = direction
    image_part(lists_ref, direction, low_ref, v0, v1, m0, m1, gram_ref, part_ref)


def last_kernel(both_ref, sol_in, res_in, dir_in, sol_ref, res_ref):
    start = pl.multiple_of(lax.axis_index("zh") * BLK, BLK)
    mine = pl.ds(start, BLK)
    both = both_ref[mine, :] + both_ref[pl.ds(start + PIECE, BLK), :]
    sol, residual, _ = advance(both, dir_in[mine, :], res_in[mine, :], sol_in[mine, :])
    sol_ref[...] = sol.astype(jnp.bfloat16)
    res_ref[...] = residual


def on_chip(kernel, args, outs, scratch=(), smem=1):
    vmem = pl.BlockSpec(memory_space=pltpu.VMEM)
    scalar = pl.BlockSpec(memory_space=pltpu.SMEM)
    return pl.pallas_call(
        kernel,
        out_shape=[jax.ShapeDtypeStruct(shape, dtype) for shape, dtype in outs],
        in_specs=[scalar] * smem + [vmem] * (len(args) - smem),
        out_specs=[vmem] * len(outs),
        scratch_shapes=list(scratch),
        compiler_params=pltpu.CompilerParams(vmem_limit_bytes=VMEM_LIMIT),
    )(*args)


def gather_stage(block, axes):
    count = 1
    for axis in axes:
        count *= SIZES[axis]
    sent = jnp.broadcast_to(block[None], (count,) + block.shape)
    return lax.all_to_all(sent, axes, 0, 0, tiled=True).reshape(-1, block.shape[1])


def in_order(block):
    held = sum(reversed(STAGES), ())
    piece = block.shape[0] // 192
    block = block.reshape(tuple(SIZES[axis] for axis in held) + (piece, block.shape[1]))
    order = tuple(held.index(axis) for axis in ROW) + (len(held), len(held) + 1)
    return block.transpose(order).reshape(-1, block.shape[-1])


def swap(value):
    return lax.ppermute(value, "core", [(0, 1), (1, 0)])


def per_device(start_rows, col_factors, block_rows, block_cols, block_masks, block_counts):
    f32, bf16 = jnp.float32, jnp.bfloat16
    core = lax.axis_index("core")
    gravity = K / (col_factors.shape[0] * 768)

    live = (jnp.arange(NB + 1) < block_counts[0, 0])[:, None, None]
    padded = jnp.pad(block_masks[0, 0], ((0, 1), (0, 0), (0, 0)))
    own_masks = jnp.where(live & (padded > 0), CONFIDENCE, 0.0).astype(bf16)
    other_masks = swap(own_masks)

    ids = jnp.concatenate(
        [block_rows[0, 0], block_cols[0, 0], jnp.broadcast_to(block_counts[0, 0], (2 * NB,))]
    )[None]
    ids = lax.all_gather(ids, "core", axis=0, tiled=True)
    lists = pl.pallas_call(
        lists_kernel,
        out_shape=jax.ShapeDtypeStruct((2 * TRIPS,), jnp.int32),
        in_specs=[pl.BlockSpec(memory_space=pltpu.SMEM)],
        out_specs=pl.BlockSpec(memory_space=pltpu.SMEM),
    )(ids)

    own = col_factors
    for axes in STAGES:
        own = gather_stage(own, axes)
    own, lists, own_masks, other_masks = lax.optimization_barrier((own, lists, own_masks, other_masks))
    own = in_order(own)
    other = swap(own)
    (own_gram,) = on_chip(gram_kernel, (own,), [((K, K), f32)], smem=0)

    rows = lax.dynamic_slice_in_dim(start_rows.reshape(2, 2, BLK, K), core, 1, 1).reshape(PIECE, K)
    big = (own, other, own_masks, other_masks)
    whole = ((PIECE, K), f32)
    low = (pltpu.VMEM((PIECE, K), bf16),)

    def both(part):
        return lax.all_gather(part, "zh", axis=0, tiled=True)

    part, gram = on_chip(
        lambda *refs: init_kernel(gravity, *refs), (lists, rows) + big + (own_gram,), [whole, ((K, K), f32)]
    )
    residual, part = on_chip(
        start_kernel, (lists, both(part), rows) + big + (gram,), [whole] * 2, low
    )
    sol, direction = rows, residual
    for _ in range(ITERS - 1):
        sol, residual, direction, part = on_chip(
            step_kernel, (lists, both(part), sol, residual, direction) + big + (gram,), [whole] * 4, low
        )
    return tuple(
        on_chip(
            last_kernel, (both(part), sol, residual, direction), [((BLK, K), bf16), ((BLK, K), f32)], smem=0
        )
    )


def solution(mesh):
    fine = Mesh(mesh.devices.reshape(tuple(SIZES.values())), tuple(SIZES))
    placed = (
        P(ROW, None),
        P(ROW + COL, None),
        P(ROW, COL, None),
        P(ROW, COL, None),
        P(ROW, COL, None, None, None),
        P(ROW, COL),
    )
    return jax.shard_map(
        per_device,
        mesh=fine,
        in_specs=placed,
        out_specs=(P(ROW + COL, None), P(ROW + COL, None)),
        check_vma=False,
    )
```

```python
import jax
import jax.numpy as jnp
from jax import lax
from jax.experimental import pallas as pl
from jax.experimental.pallas import tpu as pltpu
from jax.sharding import Mesh, PartitionSpec as P

ITERS = 3
CONFIDENCE = 2.0
REGULARIZE = 0.5
EPSILON = 1e-06

ROW = ("y4", "y2", "y1", "x2", "x1", "z3", "z1")
COL = ("zh", "core")
SIZES = {"y4": 2, "y2": 2, "y1": 2, "x2": 2, "x1": 2, "z3": 3, "z1": 2, "zh": 2, "core": 2}
STAGES = (("zh", "z3", "z1"), ("y4", "y2"), ("y1", "x2", "x1"))

BLK = 128
K = 128
NB = 32
PIECE = 2 * BLK
STRIDE = NB
TRIPS = 4 * STRIDE
HALF = BLK // 2
SHIFT = 256
VMEM_LIMIT = 40 * 1024 * 1024


def lists_kernel(own_ref, other_ref, out_ref):
    half = lax.axis_index("zh")

    def clear(i, carry):
        out_ref[i] = NB * SHIFT * SHIFT
        return carry

    lax.fori_loop(0, 4 * STRIDE, clear, 0, unroll=8)
    longest = jnp.int32(0)
    for group, ids_ref in enumerate((own_ref, other_ref)):
        side = half if group == 0 else 1 - half

        def place(slot, ends, ids_ref=ids_ref, group=group, side=side):
            low, high = ends
            row = ids_ref[slot]
            entry = slot
            for k in range(2):
                piece = 2 * ids_ref[NB + slot] + k
                chip = lax.div(piece, 3)
                y, x = chip >> 2, chip & 3
                spot = ((((y & 1) * 4 + x) * 4 + (y >> 1)) * 2 + side) * 3 + lax.rem(piece, 3)
                entry = entry * SHIFT + spot
            mine = (row >> 1) == half
            upper = (row & 1) == 1

            @pl.when(mine)
            def _():
                out_ref[jnp.where(upper, (2 * group + 1) * STRIDE + high, 2 * group * STRIDE + low)] = entry

            low = low + jnp.where(mine & jnp.logical_not(upper), 1, 0)
            high = high + jnp.where(mine & upper, 1, 0)
            return low, high

        low, high = lax.fori_loop(0, ids_ref[2 * NB], place, (jnp.int32(0), jnp.int32(0)))
        longest = jnp.maximum(longest, jnp.maximum(low, high))
    out_ref[TRIPS] = lax.div(longest + 1, 2)


def gram_of(v_ref):
    step = 2048

    def body(i, total):
        block = v_ref[pl.ds(pl.multiple_of(i * step, step), step), :]
        return total + lax.dot_general(
            block, block, (((0,), (0,)), ((), ())), preferred_element_type=jnp.float32
        )

    return lax.fori_loop(0, v_ref.shape[0] // step, body, jnp.zeros((K, K), jnp.float32))


def picked(lists_ref, v_ref, m_refs, groups, i, r, take):
    cols, masks = [], []
    for g in groups:
        for k in range(take):
            entry = lists_ref[(2 * g + r) * STRIDE + take * i + k]
            for spot in (lax.div(entry, SHIFT) & (SHIFT - 1), entry & (SHIFT - 1)):
                cols.append(v_ref[pl.ds(pl.multiple_of(spot * HALF, HALF), HALF), :])
            slot = lax.div(entry, SHIFT * SHIFT)
            mask = m_refs[g][slot & (NB - 1)]
            masks.append(jnp.where(slot < NB, mask, jnp.zeros_like(mask)))
    return jnp.concatenate(cols, axis=0), jnp.concatenate(masks, axis=1)


def weigh(rows, block, mask, opening):
    scores = lax.dot_general(
        rows, block, (((1,), (1,)), ((), ())), preferred_element_type=jnp.float32
    )
    if opening:
        scores = (1.0 + CONFIDENCE) / CONFIDENCE - scores
    return scores.astype(jnp.bfloat16) * mask


def add_sparse(lists_ref, x_ref, v_ref, m_refs, out_ref, opening, groups=(0, 1)):
    def body(i, carry):
        parts = []
        for r in range(2):
            for h in range(2):
                block, mask = picked(lists_ref, v_ref, m_refs, groups, 2 * i + h, r, 2)
                parts.append((r, block, weigh(x_ref[pl.ds(r * BLK, BLK), :], block, mask, opening)))
        for r, block, weights in parts:
            out_ref[pl.ds(r * BLK, BLK), :] += jnp.dot(
                weights, block, preferred_element_type=jnp.float32
            )
        return carry

    lax.fori_loop(0, lax.div(lists_ref[TRIPS] + 1, 2), body, 0)


def halves(a):
    high = a.astype(jnp.bfloat16)
    return high, (a - high.astype(jnp.float32)).astype(jnp.bfloat16)


def exact_dot(a, b):
    a_high, a_low = halves(a)
    b_high, b_low = halves(b)
    left = jnp.concatenate([a_high, a_high, a_low], axis=1)
    right = jnp.concatenate([b_high, b_low, b_high], axis=0)
    return jnp.dot(left, right, preferred_element_type=jnp.float32)


def early_kernel(gravity, lists_ref, x_ref, v_in, m0, v_ref, gram_ref, part_ref):
    v_ref[...] = v_in[...]
    gram = gravity * gram_of(v_in)
    gram_ref[...] = gram
    part_ref[...] = -exact_dot(x_ref[...].astype(jnp.float32), gram)
    add_sparse(lists_ref, x_ref, v_in, (m0, None), part_ref, True, (0,))


def init_kernel(lists_ref, x_ref, v_ref, m1, part_in, part_ref):
    part_ref[...] = part_in[...]
    add_sparse(lists_ref, x_ref, v_ref, (None, m1), part_ref, True, (1,))


def row_sum(a):
    return jnp.sum(a, axis=1, keepdims=True)


def advance(both, direction, residual, sol):
    image = both + REGULARIZE * direction
    norm_now = row_sum(residual * residual)
    step = norm_now / (row_sum(direction * image) + EPSILON)
    sol = sol + step * direction
    residual = residual - step * image
    return sol, residual, norm_now


def image_part(lists_ref, d, low_ref, v_ref, m0, m1, gram_ref, part_ref):
    low_ref[...] = d.astype(jnp.bfloat16)
    part_ref[...] = exact_dot(d, gram_ref[...])
    add_sparse(lists_ref, low_ref, v_ref, (m0, m1), part_ref, False)


def start_kernel(lists_ref, both_ref, x_ref, v_ref, m0, m1, gram_ref, res_ref, part_ref, low_ref):
    residual = both_ref[:PIECE] + both_ref[PIECE:] - REGULARIZE * x_ref[...].astype(jnp.float32)
    res_ref[...] = residual
    image_part(lists_ref, residual, low_ref, v_ref, m0, m1, gram_ref, part_ref)


def step_kernel(
    lists_ref, both_ref, sol_in, res_in, dir_in, v_ref, m0, m1, gram_ref,
    sol_ref, res_ref, dir_ref, part_ref, low_ref,
):
    direction = dir_in[...]
    sol, residual, norm_now = advance(
        both_ref[:PIECE] + both_ref[PIECE:], direction, res_in[...], sol_in[...].astype(jnp.float32)
    )
    sol_ref[...] = sol
    res_ref[...] = residual
    direction = residual + row_sum(residual * residual) / (norm_now + EPSILON) * direction
    dir_ref[...] = direction
    image_part(lists_ref, direction, low_ref, v_ref, m0, m1, gram_ref, part_ref)


def last_kernel(both_ref, sol_in, res_in, dir_in, sol_ref, res_ref):
    start = pl.multiple_of(lax.axis_index("core") * BLK, BLK)
    mine = pl.ds(start, BLK)
    both = both_ref[mine, :] + both_ref[pl.ds(start + PIECE, BLK), :]
    sol, residual, _ = advance(both, dir_in[mine, :], res_in[mine, :], sol_in[mine, :])
    sol_ref[...] = sol.astype(jnp.bfloat16)
    res_ref[...] = residual


def on_chip(kernel, args, outs, scratch=(), smem=1):
    vmem = pl.BlockSpec(memory_space=pltpu.VMEM)
    scalar = pl.BlockSpec(memory_space=pltpu.SMEM)
    return pl.pallas_call(
        kernel,
        out_shape=[jax.ShapeDtypeStruct(shape, dtype) for shape, dtype in outs],
        in_specs=[scalar] * smem + [vmem] * (len(args) - smem),
        out_specs=[vmem] * len(outs),
        scratch_shapes=list(scratch),
        compiler_params=pltpu.CompilerParams(vmem_limit_bytes=VMEM_LIMIT),
    )(*args)


def made_lists(ids, others):
    return pl.pallas_call(
        lists_kernel,
        out_shape=jax.ShapeDtypeStruct((2 * TRIPS,), jnp.int32),
        in_specs=[pl.BlockSpec(memory_space=pltpu.SMEM)] * 2,
        out_specs=pl.BlockSpec(memory_space=pltpu.SMEM),
    )(ids, others)


def gather_stage(block, axes):
    count = 1
    for axis in axes:
        count *= SIZES[axis]
    sent = jnp.broadcast_to(block[None], (count,) + block.shape)
    return lax.all_to_all(sent, axes, 0, 0, tiled=True).reshape(-1, block.shape[1])


def swap(value):
    return lax.ppermute(value, "zh", [(0, 1), (1, 0)])


def per_device(start_rows, col_factors, block_rows, block_cols, block_masks, block_counts):
    f32, bf16 = jnp.float32, jnp.bfloat16
    half = lax.axis_index("zh")
    gravity = K / (col_factors.shape[0] * 768)

    live = (jnp.arange(NB) < block_counts[0, 0])[:, None, None]
    own_masks = jnp.where(live & (block_masks[0, 0] > 0), CONFIDENCE, 0.0).astype(bf16)
    ids = jnp.concatenate(
        [block_rows[0, 0], block_cols[0, 0], jnp.broadcast_to(block_counts[0, 0], (2 * NB,))]
    )
    extra = jnp.broadcast_to(ids.astype(bf16)[None], (16, K))
    pieces = gather_stage(jnp.concatenate([col_factors, extra]), STAGES[0])
    pieces, own_masks = lax.optimization_barrier((pieces, own_masks))
    other_masks = swap(own_masks)
    pieces = pieces.reshape(12, 48, K)
    member = (1 - half) * 6 + lax.axis_index(("z3", "z1"))
    other_ids = lax.dynamic_index_in_dim(pieces[:, 32], member, 0, keepdims=False).astype(jnp.int32)
    pieces = pieces[:, :32].reshape(12 * 32, K)

    def gathered(pieces, ids, other_ids):
        lists = made_lists(ids, other_ids)
        for axes in STAGES[1:]:
            pieces = gather_stage(pieces, axes)
        return pieces, lists

    def nothing(pieces, ids, other_ids):
        return jnp.zeros((32 * pieces.shape[0], K), bf16), jnp.zeros((2 * TRIPS,), jnp.int32)

    rows_all, lists = lax.cond(block_counts[0, 0] > 0, gathered, nothing, pieces, ids, other_ids)
    rows = lax.dynamic_slice_in_dim(start_rows, half * PIECE, PIECE, 0)
    rows_all, gram, part = on_chip(
        lambda *refs: early_kernel(gravity, *refs), (lists, rows, rows_all, own_masks),
        [(rows_all.shape, bf16), ((K, K), f32), ((PIECE, K), f32)],
    )
    big = (rows_all, own_masks, other_masks, gram)
    whole = ((PIECE, K), f32)
    low = (pltpu.VMEM((PIECE, K), bf16),)

    def both(part):
        return lax.all_gather(part, "core", axis=0, tiled=True)

    (part,) = on_chip(init_kernel, (lists, rows, rows_all, other_masks, part), [whole])
    residual, part = on_chip(start_kernel, (lists, both(part), rows) + big, [whole] * 2, low)
    sol, direction = rows, residual
    for _ in range(ITERS - 1):
        sol, residual, direction, part = on_chip(
            step_kernel, (lists, both(part), sol, residual, direction) + big, [whole] * 4, low
        )
    return tuple(
        on_chip(
            last_kernel, (both(part), sol, residual, direction), [((BLK, K), bf16), ((BLK, K), f32)], smem=0
        )
    )


def solution(mesh):
    fine = Mesh(mesh.devices.reshape(tuple(SIZES.values())), tuple(SIZES))
    placed = (
        P(ROW, None),
        P(ROW + COL, None),
        P(ROW, COL, None),
        P(ROW, COL, None),
        P(ROW, COL, None, None, None),
        P(ROW, COL),
    )
    return jax.shard_map(
        per_device,
        mesh=fine,
        in_specs=placed,
        out_specs=(P(ROW + COL, None), P(ROW + COL, None)),
        check_vma=False,
    )
```

```python
import jax
import jax.numpy as jnp
from jax import lax
from jax.experimental import pallas as pl
from jax.experimental.pallas import tpu as pltpu
from jax.sharding import Mesh, PartitionSpec as P

ITERS = 3
CONFIDENCE = 2.0
REGULARIZE = 0.5
EPSILON = 1e-06

ROW = ("y4", "y2", "y1", "x2", "x1", "z3", "z1")
COL = ("zh", "core")
SIZES = {"y4": 2, "y2": 2, "y1": 2, "x2": 2, "x1": 2, "z3": 3, "z1": 2, "zh": 2, "core": 2}
STAGES = (("zh", "z3", "z1"), ("y4", "y2"), ("y1", "x2", "x1"))

BLK = 128
K = 128
NB = 32
PIECE = 2 * BLK
FIRST = 24
STRIDE = NB
TRIPS = 4 * STRIDE
HALF = BLK // 2
SHIFT = 256
VMEM_LIMIT = 40 * 1024 * 1024


def lists_kernel(own_ref, other_ref, out_ref):
    half = lax.axis_index("zh")

    def clear(i, carry):
        out_ref[i] = NB * SHIFT * SHIFT
        return carry

    lax.fori_loop(0, 4 * STRIDE, clear, 0, unroll=8)
    longest = sent = jnp.int32(0)
    for group, ids_ref in enumerate((own_ref, other_ref)):
        side = half if group == 0 else 1 - half

        def place(slot, ends, ids_ref=ids_ref, group=group, side=side):
            low, high = ends
            row = ids_ref[slot]
            entry = low + high
            for k in range(2):
                piece = 2 * ids_ref[NB + slot] + k
                chip = lax.div(piece, 3)
                y, x = chip >> 2, chip & 3
                spot = ((((y & 1) * 4 + x) * 4 + (y >> 1)) * 2 + side) * 3 + lax.rem(piece, 3)
                entry = entry * SHIFT + spot
            mine = (row >> 1) == half
            upper = (row & 1) == 1

            @pl.when(mine)
            def _():
                out_ref[jnp.where(upper, (2 * group + 1) * STRIDE + high, 2 * group * STRIDE + low)] = entry

            low = low + jnp.where(mine & jnp.logical_not(upper), 1, 0)
            high = high + jnp.where(mine & upper, 1, 0)
            return low, high

        count = ids_ref[2 * NB]
        low, high = lax.fori_loop(0, count, place, (jnp.int32(0), jnp.int32(0)))
        longest = jnp.maximum(longest, jnp.maximum(low, high))
        sent = jnp.maximum(sent, count - low - high if group == 0 else low + high)
    out_ref[TRIPS] = lax.div(longest + 1, 2)
    out_ref[TRIPS + 1] = sent


def sort_kernel(ids_ref, mask_ref, kept_ref, first_ref, rest_ref):
    half = lax.axis_index("zh")

    def place(slot, ends):
        kept, sent = ends
        mine = (ids_ref[slot] >> 1) == half
        block = jnp.where(mask_ref[slot] > 0, CONFIDENCE, 0.0).astype(jnp.bfloat16)

        @pl.when(mine)
        def _():
            kept_ref[kept] = block

        @pl.when(jnp.logical_not(mine) & (sent < FIRST))
        def _():
            first_ref[sent] = block

        @pl.when(jnp.logical_not(mine) & (sent >= FIRST))
        def _():
            rest_ref[sent - FIRST] = block

        return kept + jnp.where(mine, 1, 0), sent + jnp.where(mine, 0, 1)

    lax.fori_loop(0, ids_ref[2 * NB], place, (jnp.int32(0), jnp.int32(0)))


def gram_of(v_ref):
    step = 2048

    def body(i, total):
        block = v_ref[pl.ds(pl.multiple_of(i * step, step), step), :]
        return total + lax.dot_general(
            block, block, (((0,), (0,)), ((), ())), preferred_element_type=jnp.float32
        )

    return lax.fori_loop(0, v_ref.shape[0] // step, body, jnp.zeros((K, K), jnp.float32))


def picked(lists_ref, v_ref, m_refs, groups, i, r, take):
    cols, masks = [], []
    for g in groups:
        for k in range(take):
            entry = lists_ref[(2 * g + r) * STRIDE + take * i + k]
            for spot in (lax.div(entry, SHIFT) & (SHIFT - 1), entry & (SHIFT - 1)):
                cols.append(v_ref[pl.ds(pl.multiple_of(spot * HALF, HALF), HALF), :])
            slot = lax.div(entry, SHIFT * SHIFT)
            mask = m_refs[g][slot & (NB - 1)]
            masks.append(jnp.where(slot < NB, mask, jnp.zeros_like(mask)))
    return jnp.concatenate(cols, axis=0), jnp.concatenate(masks, axis=1)


def weigh(rows, block, mask, opening):
    scores = lax.dot_general(
        rows, block, (((1,), (1,)), ((), ())), preferred_element_type=jnp.float32
    )
    if opening:
        scores = (1.0 + CONFIDENCE) / CONFIDENCE - scores
    return scores.astype(jnp.bfloat16) * mask


def add_sparse(lists_ref, x_ref, v_ref, m_refs, out_ref, opening, groups=(0, 1)):
    def body(i, carry):
        parts = []
        for r in range(2):
            for h in range(2):
                block, mask = picked(lists_ref, v_ref, m_refs, groups, 2 * i + h, r, 2)
                parts.append((r, block, weigh(x_ref[pl.ds(r * BLK, BLK), :], block, mask, opening)))
        for r, block, weights in parts:
            out_ref[pl.ds(r * BLK, BLK), :] += jnp.dot(
                weights, block, preferred_element_type=jnp.float32
            )
        return carry

    lax.fori_loop(0, lax.div(lists_ref[TRIPS] + 1, 2), body, 0)


def halves(a):
    high = a.astype(jnp.bfloat16)
    return high, (a - high.astype(jnp.float32)).astype(jnp.bfloat16)


def exact_dot(a, b):
    a_high, a_low = halves(a)
    b_high, b_low = halves(b)
    left = jnp.concatenate([a_high, a_high, a_low], axis=1)
    right = jnp.concatenate([b_high, b_low, b_high], axis=0)
    return jnp.dot(left, right, preferred_element_type=jnp.float32)


def early_kernel(gravity, lists_ref, x_ref, v_in, m0, gram_ref, part_ref):
    gram = gravity * gram_of(v_in)
    gram_ref[...] = gram
    part_ref[...] = -exact_dot(x_ref[...].astype(jnp.float32), gram)
    add_sparse(lists_ref, x_ref, v_in, (m0, None), part_ref, True, (0,))


def init_kernel(lists_ref, x_ref, v_ref, first_ref, rest_ref, part_in, part_ref, m1):
    m1[:FIRST] = first_ref[...]
    m1[FIRST:] = rest_ref[...]
    part_ref[...] = part_in[...]
    add_sparse(lists_ref, x_ref, v_ref, (None, m1), part_ref, True, (1,))


def row_sum(a):
    return jnp.sum(a, axis=1, keepdims=True)


def advance(both, direction, residual, sol):
    image = both + REGULARIZE * direction
    norm_now = row_sum(residual * residual)
    step = norm_now / (row_sum(direction * image) + EPSILON)
    sol = sol + step * direction
    residual = residual - step * image
    return sol, residual, norm_now


def image_part(lists_ref, d, low_ref, v_ref, m0, m1, gram_ref, part_ref):
    low_ref[...] = d.astype(jnp.bfloat16)
    part_ref[...] = exact_dot(d, gram_ref[...])
    add_sparse(lists_ref, low_ref, v_ref, (m0, m1), part_ref, False)


def start_kernel(lists_ref, both_ref, x_ref, v_ref, m0, m1, gram_ref, res_ref, part_ref, low_ref):
    residual = both_ref[:PIECE] + both_ref[PIECE:] - REGULARIZE * x_ref[...].astype(jnp.float32)
    res_ref[...] = residual
    image_part(lists_ref, residual, low_ref, v_ref, m0, m1, gram_ref, part_ref)


def step_kernel(
    lists_ref, both_ref, sol_in, res_in, dir_in, v_ref, m0, m1, gram_ref,
    sol_ref, res_ref, dir_ref, part_ref, low_ref,
):
    direction = dir_in[...]
    sol, residual, norm_now = advance(
        both_ref[:PIECE] + both_ref[PIECE:], direction, res_in[...], sol_in[...].astype(jnp.float32)
    )
    sol_ref[...] = sol
    res_ref[...] = residual
    direction = residual + row_sum(residual * residual) / (norm_now + EPSILON) * direction
    dir_ref[...] = direction
    image_part(lists_ref, direction, low_ref, v_ref, m0, m1, gram_ref, part_ref)


def last_kernel(both_ref, sol_in, res_in, dir_in, sol_ref, res_ref):
    start = pl.multiple_of(lax.axis_index("core") * BLK, BLK)
    mine = pl.ds(start, BLK)
    both = both_ref[mine, :] + both_ref[pl.ds(start + PIECE, BLK), :]
    sol, residual, _ = advance(both, dir_in[mine, :], res_in[mine, :], sol_in[mine, :])
    sol_ref[...] = sol.astype(jnp.bfloat16)
    res_ref[...] = residual


def on_chip(kernel, args, outs, scratch=(), smem=1):
    vmem = pl.BlockSpec(memory_space=pltpu.VMEM)
    scalar = pl.BlockSpec(memory_space=pltpu.SMEM)
    return pl.pallas_call(
        kernel,
        out_shape=[jax.ShapeDtypeStruct(shape, dtype) for shape, dtype in outs],
        in_specs=[scalar] * smem + [vmem] * (len(args) - smem),
        out_specs=[vmem] * len(outs),
        scratch_shapes=list(scratch),
        compiler_params=pltpu.CompilerParams(vmem_limit_bytes=VMEM_LIMIT),
    )(*args)


def made_lists(ids, others):
    return pl.pallas_call(
        lists_kernel,
        out_shape=jax.ShapeDtypeStruct((2 * TRIPS,), jnp.int32),
        in_specs=[pl.BlockSpec(memory_space=pltpu.SMEM)] * 2,
        out_specs=pl.BlockSpec(memory_space=pltpu.SMEM),
    )(ids, others)


def gather_stage(block, axes):
    count = 1
    for axis in axes:
        count *= SIZES[axis]
    sent = jnp.broadcast_to(block[None], (count,) + block.shape)
    return lax.all_to_all(sent, axes, 0, 0, tiled=True).reshape(-1, block.shape[1])


def swap(value):
    return lax.ppermute(value, "zh", [(0, 1), (1, 0)])


def per_device(start_rows, col_factors, block_rows, block_cols, block_masks, block_counts):
    f32, bf16 = jnp.float32, jnp.bfloat16
    half = lax.axis_index("zh")
    gravity = K / (col_factors.shape[0] * 768)

    ids = jnp.concatenate(
        [block_rows[0, 0], block_cols[0, 0], jnp.broadcast_to(block_counts[0, 0], (2 * NB,))]
    )
    extra = jnp.broadcast_to(ids.astype(bf16)[None], (16, K))
    pieces = gather_stage(jnp.concatenate([col_factors, extra]), STAGES[0])
    own_masks, sent_first, sent_rest = on_chip(
        sort_kernel, (ids, block_masks[0, 0]), [((n, BLK, BLK), bf16) for n in (NB, FIRST, NB - FIRST)]
    )
    pieces, sent_first = lax.optimization_barrier((pieces, sent_first))
    pieces = pieces.reshape(12, 48, K)
    member = (1 - half) * 6 + lax.axis_index(("z3", "z1"))
    other_ids = lax.dynamic_index_in_dim(pieces[:, 32], member, 0, keepdims=False).astype(jnp.int32)
    pieces = pieces[:, :32].reshape(12 * 32, K)

    lists = made_lists(ids, other_ids)
    got_first = swap(sent_first)
    pieces, lists = lax.optimization_barrier((gather_stage(pieces, STAGES[1]), lists))

    def gathered(pieces):
        return gather_stage(pieces, STAGES[2])

    def nothing(pieces):
        return jnp.zeros((8 * pieces.shape[0], K), bf16)

    rows_all = lax.cond(block_counts[0, 0] > 0, gathered, nothing, pieces)

    rows = lax.dynamic_slice_in_dim(start_rows, half * PIECE, PIECE, 0)
    gram, part = on_chip(
        lambda *refs: early_kernel(gravity, *refs), (lists, rows, rows_all, own_masks),
        [((K, K), f32), ((PIECE, K), f32)],
    )
    whole = ((PIECE, K), f32)
    low = (pltpu.VMEM((PIECE, K), bf16),)

    def both(part):
        return lax.all_gather(part, "core", axis=0, tiled=True)

    got_first, sent_rest = lax.optimization_barrier((got_first, sent_rest))
    got_rest = lax.cond(lists[TRIPS + 1] > FIRST, swap, jnp.zeros_like, sent_rest)
    part, other_masks = on_chip(
        init_kernel, (lists, rows, rows_all, got_first, got_rest, part), [whole, ((NB, BLK, BLK), bf16)]
    )
    big = (rows_all, own_masks, other_masks, gram)
    residual, part = on_chip(start_kernel, (lists, both(part), rows) + big, [whole] * 2, low)
    sol, direction = rows, residual
    for _ in range(ITERS - 1):
        sol, residual, direction, part = on_chip(
            step_kernel, (lists, both(part), sol, residual, direction) + big, [whole] * 4, low
        )
    return tuple(
        on_chip(
            last_kernel, (both(part), sol, residual, direction), [((BLK, K), bf16), ((BLK, K), f32)], smem=0
        )
    )


def solution(mesh):
    fine = Mesh(mesh.devices.reshape(tuple(SIZES.values())), tuple(SIZES))
    placed = (
        P(ROW, None),
        P(ROW + COL, None),
        P(ROW, COL, None),
        P(ROW, COL, None),
        P(ROW, COL, None, None, None),
        P(ROW, COL),
    )
    return jax.shard_map(
        per_device,
        mesh=fine,
        in_specs=placed,
        out_specs=(P(ROW + COL, None), P(ROW + COL, None)),
        check_vma=False,
    )
```

```python
import jax
import jax.numpy as jnp
from jax import lax
from jax.experimental import pallas as pl
from jax.experimental.pallas import tpu as pltpu
from jax.sharding import Mesh, PartitionSpec as P

ITERS = 3
CONFIDENCE = 2.0
REGULARIZE = 0.5
EPSILON = 1e-06

ROW = ("y4", "y2", "y1", "x2", "x1", "z3", "z1")
COL = ("zh", "core")
SIZES = {"y4": 2, "y2": 2, "y1": 2, "x2": 2, "x1": 2, "z3": 3, "z1": 2, "zh": 2, "core": 2}
STAGES = (("zh", "z3", "z1"), ("y4", "y2"), ("y1", "x2", "x1"))

BLK = 128
K = 128
NB = 32
PIECE = 2 * BLK
FIRST = 24
STRIDE = NB
TRIPS = 4 * STRIDE
HALF = BLK // 2
SHIFT = 256
VMEM_LIMIT = 40 * 1024 * 1024


def lists_kernel(own_ref, other_ref, out_ref):
    half = lax.axis_index("zh")

    def clear(i, carry):
        out_ref[i] = NB * SHIFT * SHIFT
        return carry

    lax.fori_loop(0, 4 * STRIDE, clear, 0, unroll=8)
    longest = sent = jnp.int32(0)
    for group, ids_ref in enumerate((own_ref, other_ref)):
        side = half if group == 0 else 1 - half

        def place(slot, ends, ids_ref=ids_ref, group=group, side=side):
            low, high = ends
            row = ids_ref[slot]
            entry = low + high
            for k in range(2):
                piece = 2 * ids_ref[NB + slot] + k
                chip = lax.div(piece, 3)
                y, x = chip >> 2, chip & 3
                spot = ((((y & 1) * 4 + x) * 4 + (y >> 1)) * 2 + side) * 3 + lax.rem(piece, 3)
                entry = entry * SHIFT + spot
            mine = (row >> 1) == half
            upper = (row & 1) == 1

            @pl.when(mine)
            def _():
                out_ref[jnp.where(upper, (2 * group + 1) * STRIDE + high, 2 * group * STRIDE + low)] = entry

            low = low + jnp.where(mine & jnp.logical_not(upper), 1, 0)
            high = high + jnp.where(mine & upper, 1, 0)
            return low, high

        count = ids_ref[2 * NB]
        low, high = lax.fori_loop(0, count, place, (jnp.int32(0), jnp.int32(0)))
        longest = jnp.maximum(longest, jnp.maximum(low, high))
        sent = jnp.maximum(sent, count - low - high if group == 0 else low + high)
    out_ref[TRIPS] = lax.div(longest + 1, 2)
    out_ref[TRIPS + 1] = sent


def sort_kernel(ids_ref, mask_ref, kept_ref, first_ref, rest_ref):
    half = lax.axis_index("zh")

    def place(slot, ends):
        kept, sent = ends
        mine = (ids_ref[slot] >> 1) == half
        block = jnp.where(mask_ref[slot] > 0, CONFIDENCE, 0.0).astype(jnp.bfloat16)

        @pl.when(mine)
        def _():
            kept_ref[kept] = block

        @pl.when(jnp.logical_not(mine) & (sent < FIRST))
        def _():
            first_ref[sent] = block

        @pl.when(jnp.logical_not(mine) & (sent >= FIRST))
        def _():
            rest_ref[sent - FIRST] = block

        return kept + jnp.where(mine, 1, 0), sent + jnp.where(mine, 0, 1)

    lax.fori_loop(0, ids_ref[2 * NB], place, (jnp.int32(0), jnp.int32(0)))


def gram_of(v_ref):
    step = 2048

    def body(i, total):
        block = v_ref[pl.ds(pl.multiple_of(i * step, step), step), :]
        return total + lax.dot_general(
            block, block, (((0,), (0,)), ((), ())), preferred_element_type=jnp.float32
        )

    return lax.fori_loop(0, v_ref.shape[0] // step, body, jnp.zeros((K, K), jnp.float32))


def picked(lists_ref, v_ref, m_refs, groups, i, r, take):
    cols, masks = [], []
    for g in groups:
        for k in range(take):
            entry = lists_ref[(2 * g + r) * STRIDE + take * i + k]
            for spot in (lax.div(entry, SHIFT) & (SHIFT - 1), entry & (SHIFT - 1)):
                cols.append(v_ref[pl.ds(pl.multiple_of(spot * HALF, HALF), HALF), :])
            slot = lax.div(entry, SHIFT * SHIFT)
            mask = m_refs[g][slot & (NB - 1)]
            masks.append(jnp.where(slot < NB, mask, jnp.zeros_like(mask)))
    return jnp.concatenate(cols, axis=0), jnp.concatenate(masks, axis=1)


def weigh(rows, block, mask, opening):
    scores = lax.dot_general(
        rows, block, (((1,), (1,)), ((), ())), preferred_element_type=jnp.float32
    )
    if opening:
        scores = (1.0 + CONFIDENCE) / CONFIDENCE - scores
    return scores.astype(jnp.bfloat16) * mask


def add_sparse(lists_ref, x_ref, v_ref, m_refs, out_ref, opening, groups=(0, 1)):
    def body(i, carry):
        parts = []
        for r in range(2):
            for h in range(2):
                block, mask = picked(lists_ref, v_ref, m_refs, groups, 2 * i + h, r, 2)
                parts.append((r, block, weigh(x_ref[pl.ds(r * BLK, BLK), :], block, mask, opening)))
        for r, block, weights in parts:
            out_ref[pl.ds(r * BLK, BLK), :] += jnp.dot(
                weights, block, preferred_element_type=jnp.float32
            )
        return carry

    lax.fori_loop(0, lax.div(lists_ref[TRIPS] + 1, 2), body, 0)


def halves(a):
    high = a.astype(jnp.bfloat16)
    return high, (a - high.astype(jnp.float32)).astype(jnp.bfloat16)


def exact_dot(a, b):
    a_high, a_low = halves(a)
    b_high, b_low = halves(b)
    left = jnp.concatenate([a_high, a_high, a_low], axis=1)
    right = jnp.concatenate([b_high, b_low, b_high], axis=0)
    return jnp.dot(left, right, preferred_element_type=jnp.float32)


def early_kernel(gravity, lists_ref, x_ref, v_in, m0, gram_ref, part_ref):
    gram = gravity * gram_of(v_in)
    gram_ref[...] = gram
    part_ref[...] = -exact_dot(x_ref[...].astype(jnp.float32), gram)
    add_sparse(lists_ref, x_ref, v_in, (m0, None), part_ref, True, (0,))


def init_kernel(lists_ref, x_ref, v_ref, first_ref, rest_ref, part_in, part_ref, m1):
    m1[:FIRST] = first_ref[...]
    m1[FIRST:] = rest_ref[...]
    part_ref[...] = part_in[...]
    add_sparse(lists_ref, x_ref, v_ref, (None, m1), part_ref, True, (1,))


def row_sum(a):
    return jnp.sum(a, axis=1, keepdims=True)


def advance(both, direction, residual, sol):
    image = both + REGULARIZE * direction
    norm_now = row_sum(residual * residual)
    step = norm_now / (row_sum(direction * image) + EPSILON)
    sol = sol + step * direction
    residual = residual - step * image
    return sol, residual, norm_now


def image_part(lists_ref, d, low_ref, v_ref, m0, m1, gram_ref, part_ref):
    low_ref[...] = d.astype(jnp.bfloat16)
    part_ref[...] = exact_dot(d, gram_ref[...])
    add_sparse(lists_ref, low_ref, v_ref, (m0, m1), part_ref, False)


def start_kernel(lists_ref, both_ref, x_ref, v_ref, m0, m1, gram_ref, res_ref, part_ref, low_ref):
    residual = both_ref[:PIECE] + both_ref[PIECE:] - REGULARIZE * x_ref[...].astype(jnp.float32)
    res_ref[...] = residual
    image_part(lists_ref, residual, low_ref, v_ref, m0, m1, gram_ref, part_ref)


def step_kernel(
    lists_ref, both_ref, sol_in, res_in, dir_in, v_ref, m0, m1, gram_ref,
    sol_ref, res_ref, dir_ref, part_ref, low_ref,
):
    direction = dir_in[...]
    sol, residual, norm_now = advance(
        both_ref[:PIECE] + both_ref[PIECE:], direction, res_in[...], sol_in[...].astype(jnp.float32)
    )
    sol_ref[...] = sol
    res_ref[...] = residual
    direction = residual + row_sum(residual * residual) / (norm_now + EPSILON) * direction
    dir_ref[...] = direction
    image_part(lists_ref, direction, low_ref, v_ref, m0, m1, gram_ref, part_ref)


def last_kernel(both_ref, sol_in, res_in, dir_in, sol_ref, res_ref):
    start = pl.multiple_of(lax.axis_index("core") * BLK, BLK)
    mine = pl.ds(start, BLK)
    both = both_ref[mine, :] + both_ref[pl.ds(start + PIECE, BLK), :]
    sol, residual, _ = advance(both, dir_in[mine, :], res_in[mine, :], sol_in[mine, :])
    sol_ref[...] = sol.astype(jnp.bfloat16)
    res_ref[...] = residual


def on_chip(kernel, args, outs, scratch=(), smem=1):
    vmem = pl.BlockSpec(memory_space=pltpu.VMEM)
    scalar = pl.BlockSpec(memory_space=pltpu.SMEM)
    return pl.pallas_call(
        kernel,
        out_shape=[jax.ShapeDtypeStruct(shape, dtype) for shape, dtype in outs],
        in_specs=[scalar] * smem + [vmem] * (len(args) - smem),
        out_specs=[vmem] * len(outs),
        scratch_shapes=list(scratch),
        compiler_params=pltpu.CompilerParams(vmem_limit_bytes=VMEM_LIMIT),
    )(*args)


def made_lists(ids, others):
    return pl.pallas_call(
        lists_kernel,
        out_shape=jax.ShapeDtypeStruct((2 * TRIPS,), jnp.int32),
        in_specs=[pl.BlockSpec(memory_space=pltpu.SMEM)] * 2,
        out_specs=pl.BlockSpec(memory_space=pltpu.SMEM),
    )(ids, others)


def gather_stage(block, axes):
    count = 1
    for axis in axes:
        count *= SIZES[axis]
    sent = jnp.broadcast_to(block[None], (count,) + block.shape)
    return lax.all_to_all(sent, axes, 0, 0, tiled=True).reshape(-1, block.shape[1])


def swap(value):
    return lax.ppermute(value, "zh", [(0, 1), (1, 0)])


def per_device(start_rows, col_factors, block_rows, block_cols, block_masks, block_counts):
    f32, bf16 = jnp.float32, jnp.bfloat16
    half = lax.axis_index("zh")
    gravity = K / (col_factors.shape[0] * 768)

    ids = jnp.concatenate(
        [block_rows[0, 0], block_cols[0, 0], jnp.broadcast_to(block_counts[0, 0], (2 * NB,))]
    )
    extra = jnp.broadcast_to(ids.astype(bf16)[None], (16, K))
    pieces = gather_stage(jnp.concatenate([col_factors, extra]), STAGES[0])
    own_masks, sent_first, sent_rest = on_chip(
        sort_kernel, (ids, block_masks[0, 0]), [((n, BLK, BLK), bf16) for n in (NB, FIRST, NB - FIRST)]
    )
    pieces, sent_first = lax.optimization_barrier((pieces, sent_first))
    pieces = pieces.reshape(12, 48, K)
    member = (1 - half) * 6 + lax.axis_index(("z3", "z1"))
    other_ids = lax.dynamic_index_in_dim(pieces[:, 32], member, 0, keepdims=False).astype(jnp.int32)
    pieces = pieces[:, :32].reshape(12 * 32, K)

    lists = made_lists(ids, other_ids)
    got_first = swap(sent_first)
    needs_rest = lists[TRIPS + 1] > FIRST
    pieces, lists, needs_rest = lax.optimization_barrier((gather_stage(pieces, STAGES[1]), lists, needs_rest))

    def gathered(pieces):
        return gather_stage(pieces, STAGES[2])

    def nothing(pieces):
        return jnp.zeros((8 * pieces.shape[0], K), bf16)

    rows_all = lax.cond(block_counts[0, 0] > 0, gathered, nothing, pieces)

    rows = lax.dynamic_slice_in_dim(start_rows, half * PIECE, PIECE, 0)
    gram, part = on_chip(
        lambda *refs: early_kernel(gravity, *refs), (lists, rows, rows_all, own_masks),
        [((K, K), f32), ((PIECE, K), f32)],
    )
    whole = ((PIECE, K), f32)
    low = (pltpu.VMEM((PIECE, K), bf16),)

    def both(part):
        return lax.all_gather(part, "core", axis=0, tiled=True)

    got_first, sent_rest = lax.optimization_barrier((got_first, sent_rest))
    got_rest = lax.cond(needs_rest, swap, jnp.zeros_like, sent_rest)
    part, other_masks = on_chip(
        init_kernel, (lists, rows, rows_all, got_first, got_rest, part), [whole, ((NB, BLK, BLK), bf16)]
    )
    big = (rows_all, own_masks, other_masks, gram)
    residual, part = on_chip(start_kernel, (lists, both(part), rows) + big, [whole] * 2, low)
    sol, direction = rows, residual
    for _ in range(ITERS - 1):
        sol, residual, direction, part = on_chip(
            step_kernel, (lists, both(part), sol, residual, direction) + big, [whole] * 4, low
        )
    return tuple(
        on_chip(
            last_kernel, (both(part), sol, residual, direction), [((BLK, K), bf16), ((BLK, K), f32)], smem=0
        )
    )


def solution(mesh):
    fine = Mesh(mesh.devices.reshape(tuple(SIZES.values())), tuple(SIZES))
    placed = (
        P(ROW, None),
        P(ROW + COL, None),
        P(ROW, COL, None),
        P(ROW, COL, None),
        P(ROW, COL, None, None, None),
        P(ROW, COL),
    )
    return jax.shard_map(
        per_device,
        mesh=fine,
        in_specs=placed,
        out_specs=(P(ROW + COL, None), P(ROW + COL, None)),
        check_vma=False,
    )
```

```python
import jax
import jax.numpy as jnp
from jax import lax
from jax.experimental import pallas as pl
from jax.experimental.pallas import tpu as pltpu
from jax.sharding import Mesh, PartitionSpec as P

ITERS = 3
CONFIDENCE = 2.0
REGULARIZE = 0.5
EPSILON = 1e-06

ROW = ("y4", "y2", "y1", "x2", "x1", "z3", "z1")
COL = ("zh", "core")
SIZES = {"y4": 2, "y2": 2, "y1": 2, "x2": 2, "x1": 2, "z3": 3, "z1": 2, "zh": 2, "core": 2}
STAGES = (("zh", "z3", "z1"), ("y4", "y2"), ("y1", "x2", "x1"))

BLK = 128
K = 128
NB = 32
PIECE = 2 * BLK
FIRST = 24
STRIDE = NB
TRIPS = 4 * STRIDE
HALF = BLK // 2
SHIFT = 256
VMEM_LIMIT = 40 * 1024 * 1024


def lists_kernel(own_ref, other_ref, out_ref):
    half = lax.axis_index("zh")

    def clear(i, carry):
        out_ref[i] = NB * SHIFT * SHIFT
        return carry

    lax.fori_loop(0, 4 * STRIDE, clear, 0, unroll=8)
    longest = sent = jnp.int32(0)
    for group, ids_ref in enumerate((own_ref, other_ref)):
        side = half if group == 0 else 1 - half

        def place(slot, ends, ids_ref=ids_ref, group=group, side=side):
            low, high = ends
            row = ids_ref[slot]
            entry = low + high
            for k in range(2):
                piece = 2 * ids_ref[NB + slot] + k
                chip = lax.div(piece, 3)
                y, x = chip >> 2, chip & 3
                spot = ((((y & 1) * 4 + x) * 4 + (y >> 1)) * 2 + side) * 3 + lax.rem(piece, 3)
                entry = entry * SHIFT + spot
            mine = (row >> 1) == half
            upper = (row & 1) == 1

            @pl.when(mine)
            def _():
                out_ref[jnp.where(upper, (2 * group + 1) * STRIDE + high, 2 * group * STRIDE + low)] = entry

            low = low + jnp.where(mine & jnp.logical_not(upper), 1, 0)
            high = high + jnp.where(mine & upper, 1, 0)
            return low, high

        count = ids_ref[2 * NB]
        low, high = lax.fori_loop(0, count, place, (jnp.int32(0), jnp.int32(0)))
        longest = jnp.maximum(longest, jnp.maximum(low, high))
        sent = jnp.maximum(sent, count - low - high if group == 0 else low + high)
    out_ref[TRIPS] = lax.div(longest + 1, 2)
    out_ref[TRIPS + 1] = sent


def sort_kernel(ids_ref, mask_ref, kept_ref, first_ref, rest_ref):
    half = lax.axis_index("zh")

    def place(slot, ends):
        kept, sent = ends
        mine = (ids_ref[slot] >> 1) == half
        block = jnp.where(mask_ref[slot] > 0, CONFIDENCE, 0.0).astype(jnp.bfloat16)

        @pl.when(mine)
        def _():
            kept_ref[kept] = block

        @pl.when(jnp.logical_not(mine) & (sent < FIRST))
        def _():
            first_ref[sent] = block

        @pl.when(jnp.logical_not(mine) & (sent >= FIRST))
        def _():
            rest_ref[sent - FIRST] = block

        return kept + jnp.where(mine, 1, 0), sent + jnp.where(mine, 0, 1)

    lax.fori_loop(0, ids_ref[2 * NB], place, (jnp.int32(0), jnp.int32(0)))


def gram_of(v_ref):
    step = 2048

    def body(i, total):
        block = v_ref[pl.ds(pl.multiple_of(i * step, step), step), :]
        return total + lax.dot_general(
            block, block, (((0,), (0,)), ((), ())), preferred_element_type=jnp.float32
        )

    return lax.fori_loop(0, v_ref.shape[0] // step, body, jnp.zeros((K, K), jnp.float32))


def picked(lists_ref, v_ref, m_refs, groups, i, r, take):
    cols, masks = [], []
    for g in groups:
        for k in range(take):
            entry = lists_ref[(2 * g + r) * STRIDE + take * i + k]
            for spot in (lax.div(entry, SHIFT) & (SHIFT - 1), entry & (SHIFT - 1)):
                cols.append(v_ref[pl.ds(pl.multiple_of(spot * HALF, HALF), HALF), :])
            slot = lax.div(entry, SHIFT * SHIFT)
            mask = m_refs[g][slot & (NB - 1)]
            masks.append(jnp.where(slot < NB, mask, jnp.zeros_like(mask)))
    return jnp.concatenate(cols, axis=0), jnp.concatenate(masks, axis=1)


def weigh(rows, block, mask, opening):
    scores = lax.dot_general(
        rows, block, (((1,), (1,)), ((), ())), preferred_element_type=jnp.float32
    )
    if opening:
        scores = (1.0 + CONFIDENCE) / CONFIDENCE - scores
    return scores.astype(jnp.bfloat16) * mask


def add_sparse(lists_ref, x_ref, v_ref, m_refs, out_ref, opening, groups=(0, 1)):
    def body(i, carry):
        parts = []
        for r in range(2):
            for h in range(2):
                block, mask = picked(lists_ref, v_ref, m_refs, groups, 2 * i + h, r, 2)
                parts.append((r, block, weigh(x_ref[pl.ds(r * BLK, BLK), :], block, mask, opening)))
        for r, block, weights in parts:
            out_ref[pl.ds(r * BLK, BLK), :] += jnp.dot(
                weights, block, preferred_element_type=jnp.float32
            )
        return carry

    lax.fori_loop(0, lax.div(lists_ref[TRIPS] + 1, 2), body, 0)


def halves(a):
    high = a.astype(jnp.bfloat16)
    return high, (a - high.astype(jnp.float32)).astype(jnp.bfloat16)


def exact_dot(a, b):
    a_high, a_low = halves(a)
    b_high, b_low = halves(b)
    left = jnp.concatenate([a_high, a_high, a_low], axis=1)
    right = jnp.concatenate([b_high, b_low, b_high], axis=0)
    return jnp.dot(left, right, preferred_element_type=jnp.float32)


def early_kernel(gravity, lists_ref, x_ref, v_in, m0, gram_ref, part_ref):
    gram = gravity * gram_of(v_in)
    gram_ref[...] = gram
    part_ref[...] = -exact_dot(x_ref[...].astype(jnp.float32), gram)
    add_sparse(lists_ref, x_ref, v_in, (m0, None), part_ref, True, (0,))


def init_kernel(lists_ref, x_ref, v_ref, first_ref, rest_ref, part_in, part_ref, m1):
    m1[:FIRST] = first_ref[...]
    m1[FIRST:] = rest_ref[...]
    part_ref[...] = part_in[...]
    add_sparse(lists_ref, x_ref, v_ref, (None, m1), part_ref, True, (1,))


def row_sum(a):
    return jnp.sum(a, axis=1, keepdims=True)


def advance(both, direction, residual, sol):
    image = both + REGULARIZE * direction
    norm_now = row_sum(residual * residual)
    step = norm_now / (row_sum(direction * image) + EPSILON)
    sol = sol + step * direction
    residual = residual - step * image
    return sol, residual, norm_now


def image_part(lists_ref, d, low_ref, v_ref, m0, m1, gram_ref, part_ref):
    low_ref[...] = d.astype(jnp.bfloat16)
    part_ref[...] = exact_dot(d, gram_ref[...])
    add_sparse(lists_ref, low_ref, v_ref, (m0, m1), part_ref, False)


def start_kernel(lists_ref, both_ref, x_ref, v_ref, m0, m1, gram_ref, res_ref, part_ref, low_ref):
    residual = both_ref[:PIECE] + both_ref[PIECE:] - REGULARIZE * x_ref[...].astype(jnp.float32)
    res_ref[...] = residual
    image_part(lists_ref, residual, low_ref, v_ref, m0, m1, gram_ref, part_ref)


def step_kernel(
    lists_ref, both_ref, sol_in, res_in, dir_in, v_ref, m0, m1, gram_ref,
    sol_ref, res_ref, dir_ref, part_ref, low_ref,
):
    direction = dir_in[...]
    sol, residual, norm_now = advance(
        both_ref[:PIECE] + both_ref[PIECE:], direction, res_in[...], sol_in[...].astype(jnp.float32)
    )
    sol_ref[...] = sol
    res_ref[...] = residual
    direction = residual + row_sum(residual * residual) / (norm_now + EPSILON) * direction
    dir_ref[...] = direction
    image_part(lists_ref, direction, low_ref, v_ref, m0, m1, gram_ref, part_ref)


def last_kernel(both_ref, sol_in, res_in, dir_in, sol_ref, res_ref):
    start = pl.multiple_of(lax.axis_index("core") * BLK, BLK)
    mine = pl.ds(start, BLK)
    both = both_ref[mine, :] + both_ref[pl.ds(start + PIECE, BLK), :]
    sol, residual, _ = advance(both, dir_in[mine, :], res_in[mine, :], sol_in[mine, :])
    sol_ref[...] = sol.astype(jnp.bfloat16)
    res_ref[...] = residual


def on_chip(kernel, args, outs, scratch=(), smem=1):
    vmem = pl.BlockSpec(memory_space=pltpu.VMEM)
    scalar = pl.BlockSpec(memory_space=pltpu.SMEM)
    return pl.pallas_call(
        kernel,
        out_shape=[jax.ShapeDtypeStruct(shape, dtype) for shape, dtype in outs],
        in_specs=[scalar] * smem + [vmem] * (len(args) - smem),
        out_specs=[vmem] * len(outs),
        scratch_shapes=list(scratch),
        compiler_params=pltpu.CompilerParams(vmem_limit_bytes=VMEM_LIMIT),
    )(*args)


def made_lists(ids, others):
    return pl.pallas_call(
        lists_kernel,
        out_shape=jax.ShapeDtypeStruct((2 * TRIPS,), jnp.int32),
        in_specs=[pl.BlockSpec(memory_space=pltpu.SMEM)] * 2,
        out_specs=pl.BlockSpec(memory_space=pltpu.SMEM),
    )(ids, others)


def gather_stage(block, axes):
    count = 1
    for axis in axes:
        count *= SIZES[axis]
    sent = jnp.broadcast_to(block[None], (count,) + block.shape)
    return lax.all_to_all(sent, axes, 0, 0, tiled=True).reshape(-1, block.shape[1])


def swap(value):
    return lax.ppermute(value, "zh", [(0, 1), (1, 0)])


def per_device(start_rows, col_factors, block_rows, block_cols, block_masks, block_counts):
    f32, bf16 = jnp.float32, jnp.bfloat16
    half = lax.axis_index("zh")
    gravity = K / (col_factors.shape[0] * 768)

    ids = jnp.concatenate(
        [block_rows[0, 0], block_cols[0, 0], jnp.broadcast_to(block_counts[0, 0], (2 * NB,))]
    )
    extra = jnp.broadcast_to(ids.astype(bf16)[None], (16, K))
    pieces = gather_stage(jnp.concatenate([col_factors, extra]), STAGES[0])
    own_masks, sent_first, sent_rest = on_chip(
        sort_kernel, (ids, block_masks[0, 0]), [((n, BLK, BLK), bf16) for n in (NB, FIRST, NB - FIRST)]
    )
    pieces, sent_first = lax.optimization_barrier((pieces, sent_first))
    pieces = pieces.reshape(12, 48, K)
    member = (1 - half) * 6 + lax.axis_index(("z3", "z1"))
    other_ids = lax.dynamic_index_in_dim(pieces[:, 32], member, 0, keepdims=False).astype(jnp.int32)
    pieces = pieces[:, :32].reshape(12 * 32, K)

    lists = made_lists(ids, other_ids)
    got_first = swap(sent_first)
    needs_rest = lists[TRIPS + 1] > FIRST
    pieces, lists, needs_rest = lax.optimization_barrier((gather_stage(pieces, STAGES[1]), lists, needs_rest))

    def gathered(pieces):
        return gather_stage(pieces, STAGES[2])

    def nothing(pieces):
        return jnp.zeros((8 * pieces.shape[0], K), bf16)

    rows_all = lax.cond(block_counts[0, 0] > 0, gathered, nothing, pieces)

    rows = lax.dynamic_slice_in_dim(start_rows, half * PIECE, PIECE, 0)
    gram, part = on_chip(
        lambda *refs: early_kernel(gravity, *refs), (lists, rows, rows_all, own_masks),
        [((K, K), f32), ((PIECE, K), f32)],
    )
    whole = ((PIECE, K), f32)
    low = (pltpu.VMEM((PIECE, K), bf16),)

    def both(part):
        return lax.all_gather(part, "core", axis=0, tiled=True)

    got_first, sent_rest = lax.optimization_barrier((got_first, sent_rest))
    got_rest = lax.cond(needs_rest, swap, lambda unused: unused, sent_rest)
    part, other_masks = on_chip(
        init_kernel, (lists, rows, rows_all, got_first, got_rest, part), [whole, ((NB, BLK, BLK), bf16)]
    )
    big = (rows_all, own_masks, other_masks, gram)
    residual, part = on_chip(start_kernel, (lists, both(part), rows) + big, [whole] * 2, low)
    sol, direction = rows, residual
    for _ in range(ITERS - 1):
        sol, residual, direction, part = on_chip(
            step_kernel, (lists, both(part), sol, residual, direction) + big, [whole] * 4, low
        )
    return tuple(
        on_chip(
            last_kernel, (both(part), sol, residual, direction), [((BLK, K), bf16), ((BLK, K), f32)], smem=0
        )
    )


def solution(mesh):
    fine = Mesh(mesh.devices.reshape(tuple(SIZES.values())), tuple(SIZES))
    placed = (
        P(ROW, None),
        P(ROW + COL, None),
        P(ROW, COL, None),
        P(ROW, COL, None),
        P(ROW, COL, None, None, None),
        P(ROW, COL),
    )
    return jax.shard_map(
        per_device,
        mesh=fine,
        in_specs=placed,
        out_specs=(P(ROW + COL, None), P(ROW + COL, None)),
        check_vma=False,
    )
```
